32 devices in a mesh: row: 8 (over z, x), col: 4 (over y, core).
Axes of the slice: x: 2, y: 2, z: 4, core: 2. Of those that a mesh axis runs over, the one named last changes fastest.
Arguments:
- tokens: bfloat16 [3008, 8192], P('row', 'col'), may hold values from -6 to 6
- weight: bfloat16 [8192, 26624], P('row', 'col'), may hold values from -0.0625 to 0.0625
Outputs:
- activated: bfloat16 [3008, 26624], P('row', 'col')
The draws below stay inside these ranges and needn't reach their ends.
All inputs are finite; a program needn't handle non-finite values.
Results may differ from the reference program's by a relative error of at most 0.001.
Values may be sent and summed in bfloat16 or wider, within the bound.
A program may use at most 192 MiB of HBM per device.

```python
import jax
import jax.numpy as jnp

D = 8192
FF = 26624
TOKENS = 3008


def block_scale(rng, shape, shards, least, high):
    factor_of = 1.0
    for axis_at, blocks in shards:
        draws = jax.random.uniform(jax.random.fold_in(jax.random.fold_in(rng, 6), axis_at), (blocks,), jnp.float32, least / len(shards), high / len(shards))
        factor_of = factor_of * jnp.repeat(jnp.exp(draws), shape[axis_at] // blocks).reshape((-1,) + (1,) * (len(shape) - 1 - axis_at))
    return factor_of


def centred(key, dims, width, limit, pieces=(), kind=jnp.bfloat16):
    result = width * jax.random.normal(key, dims, jnp.float32)
    if pieces:
        result = result * block_scale(key, dims, pieces, -0.22, 0.18)
    return jnp.clip(result, -limit, limit).astype(kind)


def setup_inputs(seed: int = 0) -> dict:
    keys = jax.random.split(jax.random.key(seed), 3)
    tokens = centred(keys[0], (TOKENS, D), 1.0, 6.0, ((0, 8), (1, 4)))
    weight = centred(keys[1], (D, FF), D ** -0.5, 0.0625, ((0, 8), (1, 4)))
    return {"tokens": tokens, "weight": weight}


def reference(tokens, weight):
    preact = jnp.dot(tokens, weight, preferred_element_type=jnp.float32)
    return jax.nn.silu(preact).astype(jnp.bfloat16)
```

```python
import functools

import jax
import jax.numpy as jnp
from jax import lax
from jax.experimental import pallas as pl
from jax.experimental.pallas import tpu as pltpu
from jax.sharding import PartitionSpec as P

LANES = 128
MESH = pl.DeviceIdType.MESH
PARTS = (4, 2, 1)


def silu(v):
    return v / (1.0 + jnp.exp(-v))


def kernel(tok_ref, w_ref, o_ref, all_ref, w_a, w_b, w_c, st_a, st_b, st_c, tbuf, acc_a, acc_b, acc_c,
           tsend, trecv, wsend, wrecv, osend, orecv, local, load):
    rows = 8
    row, col = lax.axis_index("row"), lax.axis_index("col")
    z, x = row // 2, row % 2
    y, core = col // 2, col % 2
    depth = w_ref.shape[0]
    held, staged = (w_a, w_b, w_c), (st_a, st_b, st_c)
    base = sum(PARTS[:2])
    pair = 2 * base + 1

    z1 = z + 1 - 2 * (z % 2)
    half = z // 2
    near, far = 2 - half, 3 - 3 * half
    zmid = 3 - z
    inner = (z == 1) | (z == 2)
    to_z, to_mid = (z1 * 2 + x, col), (zmid * 2 + x, col)
    to_x = (z * 2 + 1 - x, col)
    to_y = (row, (1 - y) * 2 + core)
    to_core = (row, y * 2 + 1 - core)

    barrier = pltpu.get_barrier_semaphore()
    for k in range(1, rows):
        pl.semaphore_signal(barrier, inc=1, device_id=((row + k) % rows, col), device_id_type=MESH)
    pl.semaphore_signal(barrier, inc=1, device_id=to_y, device_id_type=MESH)
    pl.semaphore_signal(barrier, inc=1, device_id=to_core, device_id_type=MESH)
    pl.semaphore_wait(barrier, rows + 1)

    def tok(r, c, dst, slot, own=False):
        return pltpu.make_async_remote_copy(
            src_ref=tok_ref if own else all_ref.at[r, c],
            dst_ref=all_ref.at[r, c],
            send_sem=tsend.at[slot],
            recv_sem=trecv.at[r * 4 + c],
            device_id=dst,
            device_id_type=MESH,
        )

    zs = (z, z1, near, far)
    col_y, col_c, col_yc = (1 - y) * 2 + core, y * 2 + 1 - core, (1 - y) * 2 + 1 - core

    def z_sends(j):
        r = zs[j] * 2 + x
        own = j == 0
        if own:
            tok(r, col, to_z, 0, own).start()
        if j < 2:
            @pl.when(inner)
            def _():
                tok(r, col, to_mid, 1 + j, own).start()
        else:
            @pl.when(inner)
            def _():
                tok(r, col, to_z, 1 + j, own).start()
        tok(r, col, to_x, 5 + j, own).start()
        tok(r, col, to_y, 9 + 2 * j, own).start()
        tok(r, col, to_core, 17 + 4 * j, own).start()

    mine = pltpu.make_async_copy(tok_ref, all_ref.at[row, col], local.at[0])
    mine.start()
    z_sends(0)

    def first_col(p, part):
        at = pair * (p // 2) + (base + 1 - core) * (p % 2) + (0, PARTS[0], base)[part]
        return pl.multiple_of(at * LANES, LANES)

    def wide(p):
        return (p + core) % 2 == 0

    def when_held(part, p, run):
        if part < 2:
            run()
        else:
            pl.when(wide(p))(run)

    def w_copy(p, src, part):
        return pltpu.make_async_remote_copy(
            src_ref=w_ref.at[:, pl.ds(first_col(p, part), PARTS[part] * LANES)],
            dst_ref=held[part].at[src],
            send_sem=wsend.at[p * 3 + part],
            recv_sem=wrecv.at[src * 3 + part],
            device_id=(p, col),
            device_id_type=MESH,
        )

    def w_own(part):
        return pltpu.make_async_copy(
            w_ref.at[:, pl.ds(first_col(row, part), PARTS[part] * LANES)],
            held[part].at[row], local.at[1 + part])

    for part in (0, 2, 1):
        for k in (4, 2, 6, 3, 5, 1, 7):
            p = (row + k) % rows
            when_held(part, p, lambda p=p, part=part: w_copy(p, row, part).start())
        when_held(part, row, lambda part=part: w_own(part).start())

    for j in range(4):
        if j > 0:
            tok(zs[j] * 2 + x, col, to_z, 0).wait_recv()
            z_sends(j)
        r = zs[j] * 2 + 1 - x
        tok(r, col, to_x, 0).wait_recv()
        tok(r, col, to_y, 10 + 2 * j).start()
        tok(r, col, to_core, 19 + 4 * j).start()
    for j in range(4):
        for a in range(2):
            r = zs[j] * 2 + (x if a == 0 else 1 - x)
            tok(r, col_y, to_y, 0).wait_recv()
            tok(r, col_y, to_core, 18 + 4 * j + 2 * a).start()
    mine.wait()
    for j in range(4):
        for a in range(2):
            r = zs[j] * 2 + (x if a == 0 else 1 - x)
            tok(r, col_c, to_core, 0).wait_recv()
            tok(r, col_yc, to_core, 0).wait_recv()

    def wait_weight(part):
        for k in range(1, rows):
            p = (row + k) % rows
            when_held(part, row, lambda p=p: w_copy(row, p, part).wait_recv())
        when_held(part, row, lambda: w_own(part).wait())

    def fetch(i, slot):
        return pltpu.make_async_copy(all_ref.at[(row + 1 + i) % rows], tbuf.at[slot], load.at[slot])

    def o_copy(p, src, part):
        return pltpu.make_async_remote_copy(
            src_ref=staged[part].at[p],
            dst_ref=o_ref.at[:, pl.ds(first_col(src, part), PARTS[part] * LANES)],
            send_sem=osend.at[p * 3 + part],
            recv_sem=orecv.at[src * 3 + part],
            device_id=(p, col),
            device_id_type=MESH,
        )

    def o_own(part):
        return pltpu.make_async_copy(
            staged[part].at[row],
            o_ref.at[:, pl.ds(first_col(row, part), PARTS[part] * LANES)], local.at[4 + part])

    accs = (acc_a, acc_b, acc_c)

    def product(i, slot, part):
        r = (row + 1 + i) % rows
        acc = accs[part]
        acc[...] = jnp.zeros_like(acc)

        def add(k, _):
            block = tbuf[slot, k // 2, :, pl.ds(pl.multiple_of((k % 2) * depth, depth), depth)]
            acc[...] += jnp.dot(block, held[part][k], preferred_element_type=jnp.float32)
            return 0

        lax.fori_loop(0, rows, add, 0)
        staged[part][r] = silu(acc[...]).astype(jnp.bfloat16)

        @pl.when(i < rows - 1)
        def _():
            o_copy(r, row, part).start()

        @pl.when(i == rows - 1)
        def _():
            o_own(part).start()

    for parts in ((0, 2), (1,)):
        for part in parts:
            wait_weight(part)
        fetch(0, 0).start()

        def step(i, _):
            slot = i % 2

            @pl.when(i < rows - 1)
            def _():
                fetch(i + 1, 1 - slot).start()

            fetch(i, slot).wait()
            for part in parts:
                when_held(part, row, lambda part=part: product(i, slot, part))
            return 0

        lax.fori_loop(0, rows, step, 0)

    for part in range(3):
        for k in range(1, rows):
            p = (row + k) % rows
            when_held(part, p, lambda p=p, part=part: w_copy(p, row, part).wait_send())
            when_held(part, row, lambda p=p, part=part: o_copy(p, row, part).wait_send())
            when_held(part, p, lambda p=p, part=part: o_copy(row, p, part).wait_recv())
        when_held(part, row, lambda part=part: o_own(part).wait())
    tok(row, col, to_z, 0).wait_send()
    for slot in range(1, 5):
        @pl.when(inner)
        def _():
            tok(row, col, to_z, slot).wait_send()
    for slot in range(5, 33):
        tok(row, col, to_z, slot).wait_send()


def spread(tokens, weight):
    m, d = tokens.shape
    depth, ff = weight.shape
    bf16, f32 = jnp.bfloat16, jnp.float32
    widths = [n * LANES for n in PARTS]
    out, _ = pl.pallas_call(
        kernel,
        out_shape=(jax.ShapeDtypeStruct((m, ff), bf16), jax.ShapeDtypeStruct((8, 4, m, d), bf16)),
        in_specs=[pl.BlockSpec(memory_space=pl.ANY)] * 2,
        out_specs=[pl.BlockSpec(memory_space=pl.ANY)] * 2,
        scratch_shapes=(
            [pltpu.VMEM((8, depth, n), bf16) for n in widths]
            + [pltpu.VMEM((8, m, n), bf16) for n in widths]
            + [pltpu.VMEM((2, 4, m, d), bf16)]
            + [pltpu.VMEM((m, n), f32) for n in widths]
            + [pltpu.SemaphoreType.DMA((n,)) for n in (33, 32, 24, 24, 24, 24, 7, 2)]
        ),
        compiler_params=pltpu.CompilerParams(
            collective_id=0, has_side_effects=True, vmem_limit_bytes=56 * 2**20),
        cost_estimate=pl.CostEstimate(
            flops=2 * m * 8 * depth * ff, bytes_accessed=2 * 2 * 32 * m * d, transcendentals=m * ff),
    )(tokens, weight)
    return out


def gather(tokens, weight):
    whole_weight = lax.all_gather(weight, "row", axis=0, tiled=True)
    preact = jnp.dot(
        lax.all_gather(tokens, "col", axis=1, tiled=True),
        whole_weight,
        preferred_element_type=jnp.float32,
    )
    return jax.nn.silu(preact).astype(jnp.bfloat16)


def on_device(rows, cols, tokens, weight):
    tiles = 4 * (2 * sum(PARTS[:2]) + 1)
    fits = (rows, cols) == (8, 4) and weight.shape[1] == tiles * LANES and tokens.shape[1] == 2 * weight.shape[0]
    return (spread if fits else gather)(tokens, weight)


def solution(mesh):
    placed = (P("row", "col"), P("row", "col"))
    return jax.shard_map(
        functools.partial(on_device, mesh.shape["row"], mesh.shape["col"]),
        mesh=mesh, in_specs=placed, out_specs=P("row", "col"), check_vma=False,
    )
```

```python
import functools

import jax
import jax.numpy as jnp
from jax import lax
from jax.experimental import pallas as pl
from jax.experimental.pallas import tpu as pltpu
from jax.sharding import PartitionSpec as P

LANES = 128
MESH = pl.DeviceIdType.MESH
PARTS = (4, 2, 1)


def silu(v):
    return v / (1.0 + jnp.exp(-v))


def kernel(tok_ref, w_ref, o_ref, all_ref, w_a, w_b, w_c, st_a, st_b, st_c, tbuf, acc_a, acc_b, acc_c,
           tsend, trecv, wsend, wrecv, osend, orecv, local, load):
    rows = 8
    row, col = lax.axis_index("row"), lax.axis_index("col")
    z, x = row // 2, row % 2
    y, core = col // 2, col % 2
    depth = w_ref.shape[0]
    held, staged = (w_a, w_b, w_c), (st_a, st_b, st_c)
    base = sum(PARTS[:2])
    pair = 2 * base + 1

    z1 = z + 1 - 2 * (z % 2)
    half = z // 2
    near, far = 2 - half, 3 - 3 * half
    zmid = 3 - z
    inner = (z == 1) | (z == 2)
    to_z, to_mid = (z1 * 2 + x, col), (zmid * 2 + x, col)
    to_x = (z * 2 + 1 - x, col)
    to_y = (row, (1 - y) * 2 + core)
    to_core = (row, y * 2 + 1 - core)

    barrier = pltpu.get_barrier_semaphore()
    for k in range(1, rows):
        pl.semaphore_signal(barrier, inc=1, device_id=((row + k) % rows, col), device_id_type=MESH)
    pl.semaphore_signal(barrier, inc=1, device_id=to_y, device_id_type=MESH)
    pl.semaphore_signal(barrier, inc=1, device_id=to_core, device_id_type=MESH)
    pl.semaphore_wait(barrier, rows + 1)

    def tok(r, c, dst, slot, own=False):
        return pltpu.make_async_remote_copy(
            src_ref=tok_ref if own else all_ref.at[r, c],
            dst_ref=all_ref.at[r, c],
            send_sem=tsend.at[slot],
            recv_sem=trecv.at[r * 4 + c],
            device_id=dst,
            device_id_type=MESH,
        )

    zs = (z, z1, near, far)
    col_y, col_c, col_yc = (1 - y) * 2 + core, y * 2 + 1 - core, (1 - y) * 2 + 1 - core

    def z_sends(j):
        r = zs[j] * 2 + x
        own = j == 0

        @pl.when(inner)
        def _():
            tok(r, col, to_mid if j < 2 else to_z, 1 + j, own).start()

        if own:
            tok(r, col, to_z, 0, own).start()
        tok(r, col, to_x, 5 + j, own).start()
        tok(r, col, to_y, 9 + j, own).start()
        tok(r, col, to_core, 17 + j, own).start()

    mine = pltpu.make_async_copy(tok_ref, all_ref.at[row, col], local.at[0])
    mine.start()
    z_sends(0)

    def first_col(p, part):
        at = pair * (p // 2) + (base + 1 - core) * (p % 2) + (0, PARTS[0], base)[part]
        return pl.multiple_of(at * LANES, LANES)

    def wide(p):
        return (p + core) % 2 == 0

    def when_held(part, p, run):
        if part < 2:
            run()
        else:
            pl.when(wide(p))(run)

    def w_copy(p, src, part):
        return pltpu.make_async_remote_copy(
            src_ref=w_ref.at[:, pl.ds(first_col(p, part), PARTS[part] * LANES)],
            dst_ref=held[part].at[src],
            send_sem=wsend.at[p * 3 + part],
            recv_sem=wrecv.at[src * 3 + part],
            device_id=(p, col),
            device_id_type=MESH,
        )

    def w_own(part):
        return pltpu.make_async_copy(
            w_ref.at[:, pl.ds(first_col(row, part), PARTS[part] * LANES)],
            held[part].at[row], local.at[1 + part])

    def send_weight(parts, ks):
        for part in parts:
            for k in ks:
                p = (row + k) % rows
                when_held(part, p, lambda p=p, part=part: w_copy(p, row, part).start())

    for j in range(1, 4):
        tok(zs[j] * 2 + x, col, to_z, 0).wait_recv()
        z_sends(j)
    send_weight((0, 2), (4, 2, 6))
    for j in range(4):
        r = zs[j] * 2 + 1 - x
        tok(r, col, to_x, 0).wait_recv()
        tok(r, col, to_y, 13 + j).start()
        tok(r, col, to_core, 21 + j).start()
    send_weight((0, 2), (3, 5, 1, 7))
    send_weight((1,), (4, 3, 5, 2, 6, 1, 7))
    for part in range(3):
        when_held(part, row, lambda part=part: w_own(part).start())

    def wait_weight(part):
        for k in range(1, rows):
            p = (row + k) % rows
            when_held(part, row, lambda p=p: w_copy(row, p, part).wait_recv())
        when_held(part, row, lambda: w_own(part).wait())

    def block(i):
        late, odd = (i % 4) // 2, i % 2
        at = (1 - late) * (z + odd * (1 - 2 * (z % 2))) + late * (near + odd * (1 - 2 * half))
        other = i // 4
        return at * 2 + x + other * (1 - 2 * x)

    def fetch(i):
        slot = i % 2
        return pltpu.make_async_copy(all_ref.at[block(i)], tbuf.at[slot], load.at[slot])

    def o_copy(p, src, part):
        return pltpu.make_async_remote_copy(
            src_ref=staged[part].at[p],
            dst_ref=o_ref.at[:, pl.ds(first_col(src, part), PARTS[part] * LANES)],
            send_sem=osend.at[p * 3 + part],
            recv_sem=orecv.at[src * 3 + part],
            device_id=(p, col),
            device_id_type=MESH,
        )

    def o_own(part):
        return pltpu.make_async_copy(
            staged[part].at[row],
            o_ref.at[:, pl.ds(first_col(row, part), PARTS[part] * LANES)], local.at[4 + part])

    accs = (acc_a, acc_b, acc_c)

    def product(i, part):
        r, slot = block(i), i % 2
        acc = accs[part]
        acc[...] = jnp.zeros_like(acc)

        def add(k, _):
            piece = tbuf[slot, k // 2, :, pl.ds(pl.multiple_of((k % 2) * depth, depth), depth)]
            acc[...] += jnp.dot(piece, held[part][k], preferred_element_type=jnp.float32)
            return 0

        lax.fori_loop(0, rows, add, 0)
        staged[part][r] = silu(acc[...]).astype(jnp.bfloat16)

        @pl.when(i > 0)
        def _():
            o_copy(r, row, part).start()

        @pl.when(i == 0)
        def _():
            o_own(part).start()

    def multiply(i, parts):
        fetch(i).wait()
        for part in parts:
            when_held(part, row, lambda part=part: product(i, part))

    lag = 5

    def first(i, _):
        @pl.when(i < rows)
        def _():
            r = block(i)
            tok(r, col_y, to_y, 0).wait_recv()
            tok(r, col_y, to_core, 25 + i).start()

        @pl.when(i == lag)
        def _():
            mine.wait()
            wait_weight(0)
            wait_weight(2)

        @pl.when((i >= lag - 1) & (i < rows + lag - 1))
        def _():
            r = block(i - lag + 1)
            tok(r, col_c, to_core, 0).wait_recv()
            tok(r, col_yc, to_core, 0).wait_recv()

        @pl.when((i >= lag) & (i < rows + lag - 1))
        def _():
            fetch(i - lag + 1).start()

        @pl.when(i == lag)
        def _():
            fetch(0).start()

        @pl.when(i >= lag)
        def _():
            multiply(i - lag, (0, 2))

        return 0

    lax.fori_loop(0, rows + lag, first, 0)

    wait_weight(1)
    fetch(0).start()

    def second(i, _):
        @pl.when(i < rows - 1)
        def _():
            fetch(i + 1).start()

        multiply(i, (1,))
        return 0

    lax.fori_loop(0, rows, second, 0)

    for part in range(3):
        for k in range(1, rows):
            p = (row + k) % rows
            when_held(part, p, lambda p=p, part=part: w_copy(p, row, part).wait_send())
            when_held(part, row, lambda p=p, part=part: o_copy(p, row, part).wait_send())
            when_held(part, p, lambda p=p, part=part: o_copy(row, p, part).wait_recv())
        when_held(part, row, lambda part=part: o_own(part).wait())
    tok(row, col, to_z, 0).wait_send()
    for slot in range(1, 5):
        @pl.when(inner)
        def _():
            tok(row, col, to_z, slot).wait_send()
    for slot in range(5, 33):
        tok(row, col, to_z, slot).wait_send()


def spread(tokens, weight):
    m, d = tokens.shape
    depth, ff = weight.shape
    bf16, f32 = jnp.bfloat16, jnp.float32
    widths = [n * LANES for n in PARTS]
    out, _ = pl.pallas_call(
        kernel,
        out_shape=(jax.ShapeDtypeStruct((m, ff), bf16), jax.ShapeDtypeStruct((8, 4, m, d), bf16)),
        in_specs=[pl.BlockSpec(memory_space=pl.ANY)] * 2,
        out_specs=[pl.BlockSpec(memory_space=pl.ANY)] * 2,
        scratch_shapes=(
            [pltpu.VMEM((8, depth, n), bf16) for n in widths]
            + [pltpu.VMEM((8, m, n), bf16) for n in widths]
            + [pltpu.VMEM((2, 4, m, d), bf16)]
            + [pltpu.VMEM((m, n), f32) for n in widths]
            + [pltpu.SemaphoreType.DMA((n,)) for n in (33, 32, 24, 24, 24, 24, 7, 2)]
        ),
        compiler_params=pltpu.CompilerParams(
            collective_id=0, has_side_effects=True, vmem_limit_bytes=56 * 2**20),
        cost_estimate=pl.CostEstimate(
            flops=2 * m * 8 * depth * ff, bytes_accessed=2 * 2 * 32 * m * d, transcendentals=m * ff),
    )(tokens, weight)
    return out


def gather(tokens, weight):
    whole_weight = lax.all_gather(weight, "row", axis=0, tiled=True)
    preact = jnp.dot(
        lax.all_gather(tokens, "col", axis=1, tiled=True),
        whole_weight,
        preferred_element_type=jnp.float32,
    )
    return jax.nn.silu(preact).astype(jnp.bfloat16)


def on_device(rows, cols, tokens, weight):
    tiles = 4 * (2 * sum(PARTS[:2]) + 1)
    fits = (rows, cols) == (8, 4) and weight.shape[1] == tiles * LANES and tokens.shape[1] == 2 * weight.shape[0]
    return (spread if fits else gather)(tokens, weight)


def solution(mesh):
    placed = (P("row", "col"), P("row", "col"))
    return jax.shard_map(
        functools.partial(on_device, mesh.shape["row"], mesh.shape["col"]),
        mesh=mesh, in_specs=placed, out_specs=P("row", "col"), check_vma=False,
    )
```

```python
import functools

import jax
import jax.numpy as jnp
from jax import lax
from jax.experimental import pallas as pl
from jax.experimental.pallas import tpu as pltpu
from jax.sharding import PartitionSpec as P

LANES = 128
MESH = pl.DeviceIdType.MESH
PARTS = (5, 1, 1)


def silu(v):
    return v / (1.0 + jnp.exp(-v))


def kernel(tok_ref, w_ref, o_ref, all_ref, w_a, w_b, w_c, st_a, st_b, st_c, tbuf, acc_a, acc_b, acc_c,
           tsend, trecv, wsend, wrecv, osend, orecv, local, load):
    rows = 8
    row, col = lax.axis_index("row"), lax.axis_index("col")
    z, x = row // 2, row % 2
    y, core = col // 2, col % 2
    depth = w_ref.shape[0]
    held, staged = (w_a, w_b, w_c), (st_a, st_b, st_c)
    base = sum(PARTS[:2])
    pair = 2 * base + 1

    z1 = z + 1 - 2 * (z % 2)
    half = z // 2
    near, far = 2 - half, 3 - 3 * half
    zmid = 3 - z
    inner = (z == 1) | (z == 2)
    to_z, to_mid = (z1 * 2 + x, col), (zmid * 2 + x, col)
    to_x = (z * 2 + 1 - x, col)
    to_y = (row, (1 - y) * 2 + core)
    to_core = (row, y * 2 + 1 - core)

    barrier = pltpu.get_barrier_semaphore()
    for k in range(1, rows):
        pl.semaphore_signal(barrier, inc=1, device_id=((row + k) % rows, col), device_id_type=MESH)
    pl.semaphore_signal(barrier, inc=1, device_id=to_y, device_id_type=MESH)
    pl.semaphore_signal(barrier, inc=1, device_id=to_core, device_id_type=MESH)
    pl.semaphore_wait(barrier, rows + 1)

    def tok(r, c, dst, slot, own=False):
        return pltpu.make_async_remote_copy(
            src_ref=tok_ref if own else all_ref.at[r, c],
            dst_ref=all_ref.at[r, c],
            send_sem=tsend.at[slot],
            recv_sem=trecv.at[r * 4 + c],
            device_id=dst,
            device_id_type=MESH,
        )

    zs = (z, z1, near, far)
    col_y, col_c, col_yc = (1 - y) * 2 + core, y * 2 + 1 - core, (1 - y) * 2 + 1 - core

    def z_sends(j):
        r = zs[j] * 2 + x
        own = j == 0

        @pl.when(inner)
        def _():
            tok(r, col, to_mid if j < 2 else to_z, 1 + j, own).start()

        if own:
            tok(r, col, to_z, 0, own).start()
        tok(r, col, to_x, 5 + j, own).start()
        tok(r, col, to_y, 9 + j, own).start()
        tok(r, col, to_core, 17 + j, own).start()

    mine = pltpu.make_async_copy(tok_ref, all_ref.at[row, col], local.at[0])
    mine.start()
    z_sends(0)

    def first_col(p, part):
        at = pair * (p // 2) + (base + 1 - core) * (p % 2) + (0, PARTS[0], base)[part]
        return pl.multiple_of(at * LANES, LANES)

    def wide(p):
        return (p + core) % 2 == 0

    def when_held(part, p, run):
        if part < 2:
            run()
        else:
            pl.when(wide(p))(run)

    def w_copy(p, src, part):
        return pltpu.make_async_remote_copy(
            src_ref=w_ref.at[:, pl.ds(first_col(p, part), PARTS[part] * LANES)],
            dst_ref=held[part].at[src],
            send_sem=wsend.at[p * 3 + part],
            recv_sem=wrecv.at[src * 3 + part],
            device_id=(p, col),
            device_id_type=MESH,
        )

    def w_own(part):
        return pltpu.make_async_copy(
            w_ref.at[:, pl.ds(first_col(row, part), PARTS[part] * LANES)],
            held[part].at[row], local.at[1 + part])

    def send_weight(parts, ks):
        for part in parts:
            for k in ks:
                p = (row + k) % rows
                when_held(part, p, lambda p=p, part=part: w_copy(p, row, part).start())

    for j in range(1, 4):
        tok(zs[j] * 2 + x, col, to_z, 0).wait_recv()
        z_sends(j)
    send_weight((0, 2), (4, 2, 6))
    for j in range(4):
        r = zs[j] * 2 + 1 - x
        tok(r, col, to_x, 0).wait_recv()
        tok(r, col, to_y, 13 + j).start()
        tok(r, col, to_core, 21 + j).start()
    send_weight((0, 2), (3, 5, 1, 7))
    send_weight((1,), (4, 3, 5, 2, 6, 1, 7))
    for part in range(3):
        when_held(part, row, lambda part=part: w_own(part).start())

    def wait_weight(part):
        for k in range(1, rows):
            p = (row + k) % rows
            when_held(part, row, lambda p=p: w_copy(row, p, part).wait_recv())
        when_held(part, row, lambda: w_own(part).wait())

    def block(i):
        late, odd = (i % 4) // 2, i % 2
        at = (1 - late) * (z + odd * (1 - 2 * (z % 2))) + late * (near + odd * (1 - 2 * half))
        other = i // 4
        return at * 2 + x + other * (1 - 2 * x)

    def far_first(i):
        return i % 2 + 4 * (i % 4 // 2) + 2 * (1 - i // 4)

    def fetch(i, n):
        slot = i % 2
        return pltpu.make_async_copy(all_ref.at[block(n)], tbuf.at[slot], load.at[slot])

    def o_copy(p, src, part):
        return pltpu.make_async_remote_copy(
            src_ref=staged[part].at[p],
            dst_ref=o_ref.at[:, pl.ds(first_col(src, part), PARTS[part] * LANES)],
            send_sem=osend.at[p * 3 + part],
            recv_sem=orecv.at[src * 3 + part],
            device_id=(p, col),
            device_id_type=MESH,
        )

    def o_own(part):
        return pltpu.make_async_copy(
            staged[part].at[row],
            o_ref.at[:, pl.ds(first_col(row, part), PARTS[part] * LANES)], local.at[4 + part])

    accs = (acc_a, acc_b, acc_c)

    def product(i, n, part):
        r, slot = block(n), i % 2
        acc = accs[part]
        acc[...] = jnp.zeros_like(acc)

        def add(k, _):
            piece = tbuf[slot, k // 2, :, pl.ds(pl.multiple_of((k % 2) * depth, depth), depth)]
            acc[...] += jnp.dot(piece, held[part][k], preferred_element_type=jnp.float32)
            return 0

        lax.fori_loop(0, rows, add, 0)
        staged[part][r] = silu(acc[...]).astype(jnp.bfloat16)

        @pl.when(n > 0)
        def _():
            o_copy(r, row, part).start()

        @pl.when(n == 0)
        def _():
            o_own(part).start()

    def multiply(i, n, parts):
        fetch(i, n).wait()
        for part in parts:
            when_held(part, row, lambda part=part: product(i, n, part))

    lag = 5

    def first(i, _):
        @pl.when(i < rows)
        def _():
            r = block(i)
            tok(r, col_y, to_y, 0).wait_recv()
            tok(r, col_y, to_core, 25 + i).start()

        @pl.when(i == lag)
        def _():
            mine.wait()
            wait_weight(0)
            wait_weight(2)

        @pl.when((i >= lag - 1) & (i < rows + lag - 1))
        def _():
            r = block(i - lag + 1)
            tok(r, col_c, to_core, 0).wait_recv()
            tok(r, col_yc, to_core, 0).wait_recv()

        @pl.when((i >= lag) & (i < rows + lag - 1))
        def _():
            fetch(i - lag + 1, i - lag + 1).start()

        @pl.when(i == lag)
        def _():
            fetch(0, 0).start()

        @pl.when(i >= lag)
        def _():
            multiply(i - lag, i - lag, (0, 2))

        return 0

    lax.fori_loop(0, rows + lag, first, 0)

    fetch(0, far_first(0)).start()
    wait_weight(1)

    def second(i, _):
        @pl.when(i < rows - 1)
        def _():
            fetch(i + 1, far_first(i + 1)).start()

        multiply(i, far_first(i), (1,))
        return 0

    lax.fori_loop(0, rows, second, 0)

    for part in range(3):
        for k in range(1, rows):
            p = (row + k) % rows
            when_held(part, p, lambda p=p, part=part: w_copy(p, row, part).wait_send())
            when_held(part, row, lambda p=p, part=part: o_copy(p, row, part).wait_send())
            when_held(part, p, lambda p=p, part=part: o_copy(row, p, part).wait_recv())
        when_held(part, row, lambda part=part: o_own(part).wait())
    tok(row, col, to_z, 0).wait_send()
    for slot in range(1, 5):
        @pl.when(inner)
        def _():
            tok(row, col, to_z, slot).wait_send()
    for slot in range(5, 33):
        tok(row, col, to_z, slot).wait_send()


def spread(tokens, weight):
    m, d = tokens.shape
    depth, ff = weight.shape
    bf16, f32 = jnp.bfloat16, jnp.float32
    widths = [n * LANES for n in PARTS]
    out, _ = pl.pallas_call(
        kernel,
        out_shape=(jax.ShapeDtypeStruct((m, ff), bf16), jax.ShapeDtypeStruct((8, 4, m, d), bf16)),
        in_specs=[pl.BlockSpec(memory_space=pl.ANY)] * 2,
        out_specs=[pl.BlockSpec(memory_space=pl.ANY)] * 2,
        scratch_shapes=(
            [pltpu.VMEM((8, depth, n), bf16) for n in widths]
            + [pltpu.VMEM((8, m, n), bf16) for n in widths]
            + [pltpu.VMEM((2, 4, m, d), bf16)]
            + [pltpu.VMEM((m, n), f32) for n in widths]
            + [pltpu.SemaphoreType.DMA((n,)) for n in (33, 32, 24, 24, 24, 24, 7, 2)]
        ),
        compiler_params=pltpu.CompilerParams(
            collective_id=0, has_side_effects=True, vmem_limit_bytes=56 * 2**20),
        cost_estimate=pl.CostEstimate(
            flops=2 * m * 8 * depth * ff, bytes_accessed=2 * 2 * 32 * m * d, transcendentals=m * ff),
    )(tokens, weight)
    return out


def gather(tokens, weight):
    whole_weight = lax.all_gather(weight, "row", axis=0, tiled=True)
    preact = jnp.dot(
        lax.all_gather(tokens, "col", axis=1, tiled=True),
        whole_weight,
        preferred_element_type=jnp.float32,
    )
    return jax.nn.silu(preact).astype(jnp.bfloat16)


def on_device(rows, cols, tokens, weight):
    tiles = 4 * (2 * sum(PARTS[:2]) + 1)
    fits = (rows, cols) == (8, 4) and weight.shape[1] == tiles * LANES and tokens.shape[1] == 2 * weight.shape[0]
    return (spread if fits else gather)(tokens, weight)


def solution(mesh):
    placed = (P("row", "col"), P("row", "col"))
    return jax.shard_map(
        functools.partial(on_device, mesh.shape["row"], mesh.shape["col"]),
        mesh=mesh, in_specs=placed, out_specs=P("row", "col"), check_vma=False,
    )
```
